512 devices in a mesh: row: 16 (over z), col: 32 (over x, y, core).
Axes of the slice: x: 4, y: 4, z: 16, core: 2. Of those that a mesh axis runs over, the one named last changes fastest.
Arguments:
- slab: bfloat16 [12288, 65536], P('row', 'col'), may hold values from -6 to 6
- sketch: bfloat16 [65536, 256], P('col'), may hold values from -0.0234375 to 0.0234375
Outputs:
- basis: float32 [12288, 256], P(('row', 'col'))
- projected: float32 [256, 65536], P('row', 'col')
The draws below stay inside these ranges and needn't reach their ends.
All inputs are finite; a program needn't handle non-finite values.
Results may differ from the reference program's by a relative error of at most 0.0027.
Values may be sent and summed in bfloat16 or wider, within the bound.
No kernel may reach another device: no remote copies, remote signals or barrier semaphores. Data moves between devices by JAX's collectives and lax.ppermute only.
A program may use at most 64 MiB of HBM per device.

```python
import jax
import jax.numpy as jnp
from jax import lax

K = 256
M = 12288
NCOL = 65536


def block_levels(own_key, extent, pieces, least, largest):
    level, own = 1.0, jax.random.fold_in(own_key, 6)
    for axis_at, parts in pieces:
        heights = jnp.exp(jax.random.uniform(jax.random.fold_in(own, axis_at), (parts,), jnp.float32, least / len(pieces), largest / len(pieces)))
        level = level * jnp.repeat(heights, extent[axis_at] // parts).reshape([-1 if axis == axis_at else 1 for axis in range(len(extent))])
    return level


def normal_values(key, extent, deviation, limit, shards=(), kind=jnp.bfloat16):
    gain = block_levels(key, extent, shards, -0.22, 0.18) if shards else 1.0
    result = jax.random.normal(key, extent, jnp.float32) * deviation * gain
    return jnp.minimum(jnp.maximum(result, -limit), limit).astype(kind)


def setup_inputs(seed: int = 0) -> dict:
    streams_of = jax.random.split(jax.random.key(seed), 3)
    return {
        "slab": normal_values(streams_of[0], (M, NCOL), 1.0, 6.0, ((0, 16), (1, 32))),
        "sketch": normal_values(streams_of[1], (NCOL, K), NCOL ** -0.5, 0.0234375, ((0, 32),)),
    }


def reference(slab, sketch):
    sampled = jnp.dot(slab.astype(jnp.float32), sketch.astype(jnp.float32), preferred_element_type=jnp.float32)
    gram = jnp.dot(sampled.T.astype(jnp.float32), sampled.astype(jnp.float32), precision=lax.Precision.HIGHEST, preferred_element_type=jnp.float32)
    lower = jnp.linalg.cholesky(gram)
    basis = jax.scipy.linalg.solve_triangular(lower, sampled.T, lower=True).T
    basis_half = basis.astype(jnp.bfloat16)
    projected = jnp.dot(basis_half.T.astype(jnp.float32), slab.astype(jnp.float32), preferred_element_type=jnp.float32)
    return (basis, projected)
```

```python
import jax
import jax.numpy as jnp
from jax import lax
from jax.experimental import pallas as pl
from jax.experimental.pallas import tpu as pltpu
from jax.sharding import PartitionSpec as P

F32 = jnp.float32
F16 = jnp.float16
BF16 = jnp.bfloat16
EXACT = lax.Precision.HIGHEST
TILE = 64
GROUP = 4
SKETCH_SCALE = 128.0
SAMPLE_SCALE = 4.0
PROJ_SCALE = 128.0


def eliminate(tile, out_ref, n):
    groups = [tile[8 * g : 8 * g + 8, :] for g in range(n // 8)]
    shape = groups[0].shape
    sub = lax.broadcasted_iota(jnp.int32, shape, 0)
    for j in range(0, n, 2):
        g, s = j // 8, j % 8
        r0 = jnp.broadcast_to(groups[g][s : s + 1, :], shape)
        r1 = jnp.broadcast_to(groups[g][s + 1 : s + 2, :], shape)
        a = jnp.broadcast_to(r0[:, j : j + 1], shape)
        b = jnp.broadcast_to(r0[:, j + 1 : j + 2], shape)
        c = jnp.broadcast_to(r1[:, j + 1 : j + 2], shape)
        det = a * c - b * b
        inv = 1.0 / det
        ca, cb, cc = a * inv, b * inv, c * inv
        for h in range(g, n // 8):
            if h == g and s == 6:
                continue
            c0 = jnp.broadcast_to(groups[h][:, j : j + 1], shape)
            c1 = jnp.broadcast_to(groups[h][:, j + 1 : j + 2], shape)
            m0 = cc * c0 - cb * c1
            m1 = ca * c1 - cb * c0
            if h == g:
                live = sub > s + 1
                m0 = jnp.where(live, m0, 0.0)
                m1 = jnp.where(live, m1, 0.0)
            groups[h] = groups[h] - m0 * r0 - m1 * r1
        inv_a = 1.0 / a
        x0 = r0 * lax.rsqrt(a)
        x1 = (r1 - (b * inv_a) * r0) * lax.rsqrt(det * inv_a)
        out_ref[j : j + 1, :] = x0[0:1, :]
        out_ref[j + 1 : j + 2, :] = x1[0:1, :]


def inverse_factor_kernel(gram_ref, out_ref, aug, x_ref):
    n = gram_ref.shape[0]

    def eye(size):
        rows = lax.broadcasted_iota(jnp.int32, (size, size), 0)
        return (rows == lax.broadcasted_iota(jnp.int32, (size, size), 1)).astype(F32)

    aug[:, :n] = gram_ref[...]
    aug[:, n:] = eye(n)
    for k in range(n // TILE):
        lo, hi = k * TILE, (k + 1) * TILE
        tile = jnp.concatenate([aug[lo:hi, lo:hi], eye(TILE)], axis=1)
        eliminate(tile, x_ref, TILE)
        row = jnp.dot(x_ref[:, TILE:], aug[lo:hi, :], precision=EXACT, preferred_element_type=F32)
        out_ref[lo:hi, :] = row[:, n:]
        if hi < n:
            aug[hi:, :] = aug[hi:, :] - lax.dot_general(
                row[:, hi:n], row, (((0,), (0,)), ((), ())), precision=EXACT, preferred_element_type=F32
            )


def inverse_factor(gram):
    n = gram.shape[0]
    return pl.pallas_call(
        inverse_factor_kernel,
        out_shape=jax.ShapeDtypeStruct((n, n), F32),
        scratch_shapes=[pltpu.VMEM((n, 2 * n), F32), pltpu.VMEM((TILE, 2 * TILE), F32)],
        name="inverse_factor",
    )(gram)


def copies(x, count):
    return jnp.broadcast_to(x[None], (count, *x.shape))


def local(slab, sketch):
    rows, cols = slab.shape
    width = sketch.shape[1]
    col_size, row_size = lax.axis_size("col"), lax.axis_size("row")
    share = rows // col_size
    piece = width // col_size
    out_rows = width // row_size
    neighbours = [list(range(at, at + GROUP)) for at in range(0, row_size, GROUP)]
    with jax.named_scope("sample"):
        partial = jnp.dot(slab, sketch, preferred_element_type=F32)
        sent = (partial * SKETCH_SCALE).astype(F16).reshape(col_size, share, width)
        got = lax.all_to_all(sent, "col", 0, 0)
        own = jnp.sum(got.astype(F32), axis=0) * (1.0 / SKETCH_SCALE)
        shares = lax.all_to_all(copies((own * SAMPLE_SCALE).astype(F16), col_size), "col", 0, 0)
        sampled = shares.reshape(rows, width).astype(F32) * (1.0 / SAMPLE_SCALE)
    with jax.named_scope("gram"):
        part = lax.dot_general(sampled, sampled, (((0,), (0,)), ((), ())), precision=EXACT, preferred_element_type=F32)
        part = lax.dynamic_slice_in_dim(part, lax.axis_index("col") * piece, piece, 0)
        strip = jnp.sum(lax.all_to_all(copies(part, row_size), "row", 0, 0), axis=0)
        gram = lax.all_to_all(copies(strip, col_size), "col", 0, 0).reshape(width, width)
    with jax.named_scope("product"):
        high = sampled.astype(BF16)
        low = (sampled - high.astype(F32)).astype(BF16)
        product = lax.dot_general(high, slab, (((0,), (0,)), ((), ())), preferred_element_type=F32)
        product = product + lax.dot_general(low, slab, (((0,), (0,)), ((), ())), preferred_element_type=F32)
        product = product.reshape(width, GROUP, cols // GROUP).transpose(1, 0, 2)
        product = jnp.sum(lax.all_to_all(product, "row", 0, 0, axis_index_groups=neighbours), axis=0)
    with jax.named_scope("factor"):
        inverse = inverse_factor(gram)
    with jax.named_scope("basis"):
        basis = lax.dot_general(own, inverse, (((1,), (1,)), ((), ())), precision=EXACT, preferred_element_type=F32)
    with jax.named_scope("projected"):
        mine = jnp.dot(inverse, product, precision=EXACT, preferred_element_type=F32)
        sent = (mine * PROJ_SCALE).astype(F16).reshape(row_size, out_rows, cols // GROUP)
        got = lax.all_to_all(sent, "row", 0, 0).reshape(row_size // GROUP, GROUP, out_rows, cols // GROUP)
        projected = jnp.sum(got.astype(F32), axis=0) * (1.0 / PROJ_SCALE)
        projected = projected.transpose(1, 0, 2).reshape(out_rows, cols)
    return (basis, projected)


def solution(mesh):
    return jax.shard_map(
        local,
        mesh=mesh,
        in_specs=(P("row", "col"), P("col", None)),
        out_specs=(P(("row", "col"), None), P("row", "col")),
        check_vma=False,
    )
```

```python
import jax
import jax.numpy as jnp
from jax import lax
from jax.experimental import pallas as pl
from jax.experimental.pallas import tpu as pltpu
from jax.sharding import PartitionSpec as P

F32 = jnp.float32
F16 = jnp.float16
BF16 = jnp.bfloat16
EXACT = lax.Precision.HIGHEST
TILE = 64
GROUP = 4
SKETCH_SCALE = 128.0
SAMPLE_SCALE = 4.0
PROJ_SCALE = 128.0


def eliminate(tile, out_ref, n):
    groups = [tile[8 * g : 8 * g + 8, :] for g in range(n // 8)]
    shape = groups[0].shape
    spread = lambda v: jnp.broadcast_to(v, shape)
    for g in range(n // 8):
        j = 8 * g
        later = range(g + 1, n // 8)
        own = [spread(groups[g][:, j + k : j + k + 1]) for k in range(8)]
        cols = {h: [spread(groups[h][:, j + k : j + k + 1]) for k in range(8)] for h in later}
        s = [[spread(own[k][i : i + 1, :]) for k in range(i + 1)] for i in range(8)]
        rows = [spread(groups[g][i : i + 1, :]) for i in range(8)]
        for k in range(0, 8, 2):
            a, b, c = s[k][k], s[k + 1][k], s[k + 1][k + 1]
            det = a * c - b * b
            inv = 1.0 / det
            pa, pb, pc = a * inv, b * inv, c * inv
            for i in range(k + 2, 8):
                m0 = pc * s[i][k] - pb * s[i][k + 1]
                m1 = pa * s[i][k + 1] - pb * s[i][k]
                for m in range(k + 2, i + 1):
                    s[i][m] = s[i][m] - (m0 * s[m][k] + m1 * s[m][k + 1])
                rows[i] = rows[i] - (m0 * rows[k] + m1 * rows[k + 1])
            for h in later:
                m0 = pc * cols[h][k] - pb * cols[h][k + 1]
                m1 = pa * cols[h][k + 1] - pb * cols[h][k]
                for m in range(k + 2, 8):
                    cols[h][m] = cols[h][m] - (m0 * s[m][k] + m1 * s[m][k + 1])
                groups[h] = groups[h] - (m0 * rows[k] + m1 * rows[k + 1])
            inv_a = 1.0 / a
            x0 = rows[k] * lax.rsqrt(a)
            x1 = (rows[k + 1] - (b * inv_a) * rows[k]) * lax.rsqrt(det * inv_a)
            out_ref[j + k : j + k + 1, :] = x0[0:1, :]
            out_ref[j + k + 1 : j + k + 2, :] = x1[0:1, :]


def eye(size):
    rows = lax.broadcasted_iota(jnp.int32, (size, size), 0)
    return (rows == lax.broadcasted_iota(jnp.int32, (size, size), 1)).astype(F32)


def factor_kernel(gram_ref, own_ref, mine_ref, left_ref, right_ref, up_ref, down_ref, basis_ref, proj_ref, aug, x_ref, inv):
    n = gram_ref.shape[0]
    half = n // 2
    aug[:, :n] = gram_ref[...]
    aug[:, n:] = eye(n)
    for k in range(n // TILE):
        lo, hi = k * TILE, (k + 1) * TILE
        tile = jnp.concatenate([aug[lo:hi, lo:hi], eye(TILE)], axis=1)
        eliminate(tile, x_ref, TILE)
        row = jnp.dot(x_ref[:, TILE:], aug[lo:hi, :], precision=EXACT, preferred_element_type=F32)
        inv[lo:hi, :] = row[:, n:]
        if hi < n:
            aug[hi:, :] = aug[hi:, :] - lax.dot_general(
                row[:, hi:n], row, (((0,), (0,)), ((), ())), precision=EXACT, preferred_element_type=F32
            )
    total = mine_ref[...] + left_ref[...] + right_ref[...]
    total = total + jnp.concatenate([up_ref[...], down_ref[...]], axis=0)
    proj_ref[...] = jnp.dot(inv[...], total, precision=EXACT, preferred_element_type=F32) * PROJ_SCALE
    basis_ref[...] = lax.dot_general(
        own_ref[...], inv[...], (((1,), (1,)), ((), ())), precision=EXACT, preferred_element_type=F32
    )


def factor_and_apply(gram, own, parts):
    n = gram.shape[0]
    return pl.pallas_call(
        factor_kernel,
        out_shape=(jax.ShapeDtypeStruct(own.shape, F32), jax.ShapeDtypeStruct(parts[0].shape, F32)),
        scratch_shapes=[pltpu.VMEM((n, 2 * n), F32), pltpu.VMEM((TILE, 2 * TILE), F32), pltpu.VMEM((n, n), F32)],
        compiler_params=pltpu.CompilerParams(vmem_limit_bytes=32 * 2**20),
        cost_estimate=pl.CostEstimate(flops=2 * 10**9, bytes_accessed=4 * 2**20, transcendentals=0),
        name="factor_and_apply",
    )(gram, own, *parts)


def product_kernel(sampled_ref, slab_ref, mine_ref, right_ref, left_ref, far_up_ref, far_down_ref):
    width = mine_ref.shape[1]
    half = mine_ref.shape[0] // 2
    at = lax.axis_index("row")
    sampled = sampled_ref[...]
    high = sampled.astype(BF16)
    low = (sampled - high.astype(F32)).astype(BF16)
    terms = jnp.concatenate([high, low], axis=1)

    def quarter(step):
        start = pl.multiple_of(lax.rem(at + step, GROUP) * width, width)
        both = lax.dot_general(
            terms, slab_ref[:, pl.ds(start, width)], (((0,), (0,)), ((), ())), preferred_element_type=F32
        )
        return both[: 2 * half] + both[2 * half :]

    mine_ref[...] = quarter(0)
    right_ref[...] = quarter(1)
    left_ref[...] = quarter(GROUP - 1)
    far = quarter(2)
    far_up_ref[...] = far[:half]
    far_down_ref[...] = far[half:]


def product_quarters(sampled, slab):
    n, width = sampled.shape[1], slab.shape[1] // GROUP
    whole = jax.ShapeDtypeStruct((n, width), F32)
    part = jax.ShapeDtypeStruct((n // 2, width), F32)
    return pl.pallas_call(
        product_kernel,
        out_shape=(whole, whole, whole, part, part),
        compiler_params=pltpu.CompilerParams(vmem_limit_bytes=32 * 2**20),
        cost_estimate=pl.CostEstimate(flops=16 * 10**8, bytes_accessed=6 * 2**20, transcendentals=0),
        name="product_quarters",
    )(sampled, slab)


def shift(x, step):
    size = lax.axis_size("row")
    return lax.ppermute(x, "row", [(i, (i + step) % size) for i in range(size)])


def copies(x, count):
    return jnp.broadcast_to(x[None], (count, *x.shape))


def local(slab, sketch):
    rows, cols = slab.shape
    width = sketch.shape[1]
    col_size, row_size = lax.axis_size("col"), lax.axis_size("row")
    share = rows // col_size
    piece = width // col_size
    out_rows = width // row_size
    with jax.named_scope("sample"):
        partial = jnp.dot(slab, sketch, preferred_element_type=F32)
        sent = (partial * SKETCH_SCALE).astype(F16).reshape(col_size, share, width)
        got = lax.all_to_all(sent, "col", 0, 0)
        own = jnp.sum(got.astype(F32), axis=0) * (1.0 / SKETCH_SCALE)
        shares = lax.all_to_all(copies((own * SAMPLE_SCALE).astype(F16), col_size), "col", 0, 0)
        sampled = shares.reshape(rows, width).astype(F32) * (1.0 / SAMPLE_SCALE)
    with jax.named_scope("gram"):
        part = lax.dot_general(sampled, sampled, (((0,), (0,)), ((), ())), precision=EXACT, preferred_element_type=F32)
        part = lax.dynamic_slice_in_dim(part, lax.axis_index("col") * piece, piece, 0)
        strip = jnp.sum(lax.all_to_all(copies(part, row_size), "row", 0, 0), axis=0)
        gram = lax.all_to_all(copies(strip, col_size), "col", 0, 0).reshape(width, width)
    with jax.named_scope("product"):
        mine, right, left, far_up, far_down = product_quarters(sampled, slab)
        parts = (mine, shift(right, 1), shift(left, -1), shift(far_up, 2), shift(far_down, -2))
    with jax.named_scope("factor"):
        basis, sent = factor_and_apply(gram, own, parts)
    with jax.named_scope("projected"):
        sent = sent.astype(F16).reshape(row_size, out_rows, cols // GROUP)
        got = lax.all_to_all(sent, "row", 0, 0).reshape(row_size // GROUP, GROUP, out_rows, cols // GROUP)
        projected = jnp.sum(got.astype(F32), axis=0) * (1.0 / PROJ_SCALE)
        projected = projected.transpose(1, 0, 2).reshape(out_rows, cols)
    return (basis, projected)


def solution(mesh):
    return jax.shard_map(
        local,
        mesh=mesh,
        in_specs=(P("row", "col"), P("col", None)),
        out_specs=(P(("row", "col"), None), P("row", "col")),
        check_vma=False,
    )
```

```python
import jax
import jax.numpy as jnp
from jax import lax
from jax.experimental import pallas as pl
from jax.experimental.pallas import tpu as pltpu
from jax.sharding import PartitionSpec as P

F32 = jnp.float32
F16 = jnp.float16
BF16 = jnp.bfloat16
EXACT = lax.Precision.HIGHEST
TILE = 64
GROUP = 4
SKETCH_SCALE = 128.0
SAMPLE_SCALE = 4.0
PROJ_SCALE = 128.0


def eliminate(tile, out_ref, n):
    groups = [tile[8 * g : 8 * g + 8, :] for g in range(n // 8)]
    shape = groups[0].shape
    spread = lambda v: jnp.broadcast_to(v, shape)
    for g in range(n // 8):
        j = 8 * g
        later = range(g + 1, n // 8)
        own = [spread(groups[g][:, j + k : j + k + 1]) for k in range(8)]
        cols = {h: [spread(groups[h][:, j + k : j + k + 1]) for k in range(8)] for h in later}
        s = [[spread(own[k][i : i + 1, :]) for k in range(i + 1)] for i in range(8)]
        rows = [spread(groups[g][i : i + 1, :]) for i in range(8)]
        for k in range(0, 8, 2):
            a, b, c = s[k][k], s[k + 1][k], s[k + 1][k + 1]
            det = a * c - b * b
            inv = 1.0 / det
            pa, pb, pc = a * inv, b * inv, c * inv
            for i in range(k + 2, 8):
                m0 = pc * s[i][k] - pb * s[i][k + 1]
                m1 = pa * s[i][k + 1] - pb * s[i][k]
                for m in range(k + 2, i + 1):
                    s[i][m] = s[i][m] - (m0 * s[m][k] + m1 * s[m][k + 1])
                rows[i] = rows[i] - (m0 * rows[k] + m1 * rows[k + 1])
            for h in later:
                m0 = pc * cols[h][k] - pb * cols[h][k + 1]
                m1 = pa * cols[h][k + 1] - pb * cols[h][k]
                for m in range(k + 2, 8):
                    cols[h][m] = cols[h][m] - (m0 * s[m][k] + m1 * s[m][k + 1])
                groups[h] = groups[h] - (m0 * rows[k] + m1 * rows[k + 1])
            inv_a = 1.0 / a
            x0 = rows[k] * lax.rsqrt(a)
            x1 = (rows[k + 1] - (b * inv_a) * rows[k]) * lax.rsqrt(det * inv_a)
            out_ref[j + k : j + k + 1, :] = x0[0:1, :]
            out_ref[j + k + 1 : j + k + 2, :] = x1[0:1, :]


def eye(size):
    rows = lax.broadcasted_iota(jnp.int32, (size, size), 0)
    return (rows == lax.broadcasted_iota(jnp.int32, (size, size), 1)).astype(F32)


def factor_kernel(gram_ref, inv_ref, aug, x_ref):
    n = gram_ref.shape[0]
    aug[:, :n] = gram_ref[...]
    aug[:, n:] = eye(n)
    for k in range(n // TILE):
        lo, hi = k * TILE, (k + 1) * TILE
        tile = jnp.concatenate([aug[lo:hi, lo:hi], eye(TILE)], axis=1)
        eliminate(tile, x_ref, TILE)
        row = jnp.dot(x_ref[:, TILE:], aug[lo:hi, :], precision=EXACT, preferred_element_type=F32)
        inv_ref[lo:hi, :] = row[:, n:]
        if hi < n:
            aug[hi:, :] = aug[hi:, :] - lax.dot_general(
                row[:, hi:n], row, (((0,), (0,)), ((), ())), precision=EXACT, preferred_element_type=F32
            )


def inverse_factor(gram):
    n = gram.shape[0]
    return pl.pallas_call(
        factor_kernel,
        out_shape=jax.ShapeDtypeStruct((n, n), F32),
        scratch_shapes=[pltpu.VMEM((n, 2 * n), F32), pltpu.VMEM((TILE, 2 * TILE), F32)],
        compiler_params=pltpu.CompilerParams(vmem_limit_bytes=16 * 2**20),
        cost_estimate=pl.CostEstimate(flops=10**8, bytes_accessed=2**20, transcendentals=0),
        name="inverse_factor",
    )(gram)


def apply_kernel(inv_ref, mine_ref, left_ref, right_ref, up_ref, down_ref, proj_ref):
    half = up_ref.shape[0]
    near = mine_ref[...] + left_ref[...] + right_ref[...]
    total = jnp.concatenate([near[:half] + up_ref[...], near[half:] + down_ref[...]], axis=0)
    proj_ref[...] = jnp.dot(inv_ref[...], total, precision=EXACT, preferred_element_type=F32) * PROJ_SCALE


def apply_inverse(inverse, parts):
    return pl.pallas_call(
        apply_kernel,
        out_shape=jax.ShapeDtypeStruct(parts[0].shape, F32),
        compiler_params=pltpu.CompilerParams(vmem_limit_bytes=16 * 2**20),
        cost_estimate=pl.CostEstimate(flops=6 * 10**8, bytes_accessed=3 * 2**20, transcendentals=0),
        name="apply_inverse",
    )(inverse, *parts)


def product_kernel(at_ref, sampled_ref, slab_ref, mine_ref, right_ref, left_ref, far_up_ref, far_down_ref, terms):
    n, half = mine_ref.shape[0], far_up_ref.shape[0]
    step = pl.program_id(0)

    @pl.when(step == 0)
    def _():
        high = sampled_ref[...].astype(BF16)
        terms[:, :n] = high
        terms[:, n:] = (sampled_ref[...] - high.astype(F32)).astype(BF16)

    both = lax.dot_general(terms[...], slab_ref[...], (((0,), (0,)), ((), ())), preferred_element_type=F32)
    total = both[:n] + both[n:]

    @pl.when(step == 0)
    def _():
        right_ref[...] = total

    @pl.when(step == 1)
    def _():
        far_up_ref[...] = total[:half]
        far_down_ref[...] = total[half:]

    @pl.when(step == 2)
    def _():
        left_ref[...] = total

    @pl.when(step == 3)
    def _():
        mine_ref[...] = total


def product_quarters(sampled, slab):
    rows, n = sampled.shape
    width = slab.shape[1] // GROUP
    whole = jax.ShapeDtypeStruct((n, width), F32)
    part = jax.ShapeDtypeStruct((n // 2, width), F32)
    whole_spec = pl.BlockSpec((n, width), lambda step, at: (0, 0))
    part_spec = pl.BlockSpec((n // 2, width), lambda step, at: (0, 0))
    at = lax.axis_index("row").astype(jnp.int32).reshape(1)
    return pl.pallas_call(
        product_kernel,
        out_shape=(whole, whole, whole, part, part),
        grid_spec=pltpu.PrefetchScalarGridSpec(
            num_scalar_prefetch=1,
            grid=(GROUP,),
            in_specs=[
                pl.BlockSpec((rows, n), lambda step, at: (0, 0)),
                pl.BlockSpec((rows, width), lambda step, at: (0, lax.rem(at[0] + step + 1, GROUP))),
            ],
            out_specs=(whole_spec, whole_spec, whole_spec, part_spec, part_spec),
            scratch_shapes=[pltpu.VMEM((rows, 2 * n), BF16)],
        ),
        compiler_params=pltpu.CompilerParams(vmem_limit_bytes=60 * 2**20),
        cost_estimate=pl.CostEstimate(flops=16 * 10**8, bytes_accessed=6 * 2**20, transcendentals=0),
        name="product_quarters",
    )(at, sampled, slab)


def shift(x, step):
    size = lax.axis_size("row")
    return lax.ppermute(x, "row", [(i, (i + step) % size) for i in range(size)])


def copies(x, count):
    return jnp.broadcast_to(x[None], (count, *x.shape))


def local(slab, sketch):
    rows, cols = slab.shape
    width = sketch.shape[1]
    col_size, row_size = lax.axis_size("col"), lax.axis_size("row")
    share = rows // col_size
    piece = width // col_size
    out_rows = width // row_size
    with jax.named_scope("sample"):
        partial = jnp.dot(slab, sketch, preferred_element_type=F32)
        sent = (partial * SKETCH_SCALE).astype(F16).reshape(col_size, share, width)
        got = lax.all_to_all(sent, "col", 0, 0)
        own = jnp.sum(got.astype(F32), axis=0) * (1.0 / SKETCH_SCALE)
        shares = lax.all_to_all(copies((own * SAMPLE_SCALE).astype(F16), col_size), "col", 0, 0)
        sampled = shares.reshape(rows, width).astype(F32) * (1.0 / SAMPLE_SCALE)
    with jax.named_scope("gram"):
        part = lax.dot_general(sampled, sampled, (((0,), (0,)), ((), ())), precision=EXACT, preferred_element_type=F32)
        part = lax.dynamic_slice_in_dim(part, lax.axis_index("col") * piece, piece, 0)
        strip = jnp.sum(lax.all_to_all(copies(part, row_size), "row", 0, 0), axis=0)
    with jax.named_scope("product"):
        mine, right, left, far_up, far_down = product_quarters(sampled, slab)
        near = (mine, shift(right, 1), shift(left, -1))
        far_up, far_down, strip = lax.optimization_barrier((far_up, far_down, strip))
        parts = near + (shift(far_up, 2), shift(far_down, -2))
    with jax.named_scope("gram"):
        gram = lax.all_to_all(copies(strip, col_size), "col", 0, 0).reshape(width, width)
    with jax.named_scope("factor"):
        inverse = inverse_factor(gram)
    with jax.named_scope("basis"):
        basis = lax.dot_general(own, inverse, (((1,), (1,)), ((), ())), precision=EXACT, preferred_element_type=F32)
    with jax.named_scope("projected"):
        sent = apply_inverse(inverse, parts).astype(F16).reshape(row_size, out_rows, cols // GROUP)
        got = lax.all_to_all(sent, "row", 0, 0).reshape(row_size // GROUP, GROUP, out_rows, cols // GROUP)
        projected = jnp.sum(got.astype(F32), axis=0) * (1.0 / PROJ_SCALE)
        projected = projected.transpose(1, 0, 2).reshape(out_rows, cols)
    return (basis, projected)


def solution(mesh):
    return jax.shard_map(
        local,
        mesh=mesh,
        in_specs=(P("row", "col"), P("col", None)),
        out_specs=(P(("row", "col"), None), P("row", "col")),
        check_vma=False,
    )
```

```python
import jax
import jax.numpy as jnp
from jax import lax
from jax.experimental import pallas as pl
from jax.experimental.pallas import tpu as pltpu
from jax.sharding import PartitionSpec as P

F32 = jnp.float32
F16 = jnp.float16
BF16 = jnp.bfloat16
EXACT = lax.Precision.HIGHEST
TILE = 64
LANES = 128
PRODUCT_MIB = 50
GROUP = 4
SKETCH_SCALE = 128.0
SAMPLE_SCALE = 4.0
PROJ_SCALE = 128.0


def eliminate(tile, out_ref, n):
    groups = [tile[8 * g : 8 * g + 8, :] for g in range(n // 8)]
    shape = groups[0].shape
    spread = lambda v: jnp.broadcast_to(v, shape)
    for g in range(n // 8):
        j = 8 * g
        later = range(g + 1, n // 8)
        own = [spread(groups[g][:, j + k : j + k + 1]) for k in range(8)]
        cols = {h: [spread(groups[h][:, j + k : j + k + 1]) for k in range(8)] for h in later}
        s = [[spread(own[k][i : i + 1, :]) for k in range(i + 1)] for i in range(8)]
        rows = [spread(groups[g][i : i + 1, :]) for i in range(8)]
        for k in range(0, 8, 2):
            a, b, c = s[k][k], s[k + 1][k], s[k + 1][k + 1]
            det = a * c - b * b
            inv = 1.0 / det
            pa, pb, pc = a * inv, b * inv, c * inv
            for i in range(k + 2, 8):
                m0 = pc * s[i][k] - pb * s[i][k + 1]
                m1 = pa * s[i][k + 1] - pb * s[i][k]
                for m in range(k + 2, i + 1):
                    s[i][m] = s[i][m] - (m0 * s[m][k] + m1 * s[m][k + 1])
                rows[i] = rows[i] - (m0 * rows[k] + m1 * rows[k + 1])
            for h in later:
                m0 = pc * cols[h][k] - pb * cols[h][k + 1]
                m1 = pa * cols[h][k + 1] - pb * cols[h][k]
                for m in range(k + 2, 8):
                    cols[h][m] = cols[h][m] - (m0 * s[m][k] + m1 * s[m][k + 1])
                groups[h] = groups[h] - (m0 * rows[k] + m1 * rows[k + 1])
            inv_a = 1.0 / a
            x0 = rows[k] * lax.rsqrt(a)
            x1 = (rows[k + 1] - (b * inv_a) * rows[k]) * lax.rsqrt(det * inv_a)
            out_ref[j + k : j + k + 1, :] = x0[0:1, :]
            out_ref[j + k + 1 : j + k + 2, :] = x1[0:1, :]


def eye(size):
    rows = lax.broadcasted_iota(jnp.int32, (size, size), 0)
    return (rows == lax.broadcasted_iota(jnp.int32, (size, size), 1)).astype(F32)


def factor_kernel(gram_ref, inv_ref, aug, x_ref):
    n = gram_ref.shape[0]
    aug[:, :n] = gram_ref[...]
    aug[:, n:] = eye(n)
    for k in range(n // TILE):
        lo, hi = k * TILE, (k + 1) * TILE
        tile = jnp.concatenate([aug[lo:hi, lo:hi], eye(TILE)], axis=1)
        eliminate(tile, x_ref, TILE)
        first, last = hi // LANES * LANES, n + pl.cdiv(hi, LANES) * LANES
        row = jnp.dot(x_ref[:, TILE:], aug[lo:hi, first:last], precision=EXACT, preferred_element_type=F32)
        inv_ref[lo:hi, : last - n] = row[:, n - first :]
        if last < 2 * n:
            inv_ref[lo:hi, last - n :] = jnp.zeros((TILE, 2 * n - last), F32)
        if hi < n:
            aug[hi:, first:last] = aug[hi:, first:last] - lax.dot_general(
                row[:, hi - first : n - first], row, (((0,), (0,)), ((), ())), precision=EXACT, preferred_element_type=F32
            )


def inverse_factor(gram):
    n = gram.shape[0]
    return pl.pallas_call(
        factor_kernel,
        out_shape=jax.ShapeDtypeStruct((n, n), F32),
        scratch_shapes=[pltpu.VMEM((n, 2 * n), F32), pltpu.VMEM((TILE, 2 * TILE), F32)],
        compiler_params=pltpu.CompilerParams(vmem_limit_bytes=16 * 2**20),
        cost_estimate=pl.CostEstimate(flops=10**8, bytes_accessed=2**20, transcendentals=0),
        name="inverse_factor",
    )(gram)


def apply_kernel(inv_ref, mine_ref, left_ref, right_ref, up_ref, down_ref, proj_ref):
    half = up_ref.shape[0]
    near = mine_ref[...] + left_ref[...] + right_ref[...]
    total = jnp.concatenate([near[:half] + up_ref[...], near[half:] + down_ref[...]], axis=0)
    proj_ref[...] = jnp.dot(inv_ref[...], total, precision=EXACT, preferred_element_type=F32) * PROJ_SCALE


def apply_inverse(inverse, parts):
    return pl.pallas_call(
        apply_kernel,
        out_shape=jax.ShapeDtypeStruct(parts[0].shape, F32),
        compiler_params=pltpu.CompilerParams(vmem_limit_bytes=16 * 2**20),
        cost_estimate=pl.CostEstimate(flops=6 * 10**8, bytes_accessed=3 * 2**20, transcendentals=0),
        name="apply_inverse",
    )(inverse, *parts)


def product_kernel(sampled_ref, slab_ref, mine_ref, right_ref, left_ref, far_up_ref, far_down_ref, held, sems):
    half, width = far_up_ref.shape
    at = lax.axis_index("row")

    def load(step):
        start = pl.multiple_of(lax.rem(at + step, GROUP) * width, width)
        return pltpu.make_async_copy(slab_ref.at[:, pl.ds(start, width)], held.at[step], sems.at[step])

    order = (1, 3, 2, 0)
    for step in order:
        load(step).start()
    sampled = sampled_ref[...].T
    high = sampled.astype(BF16)
    low = (sampled - high.astype(F32)).astype(BF16)

    def quarter(step):
        load(step).wait()
        total = jnp.dot(high, held[step], preferred_element_type=F32)
        return total + jnp.dot(low, held[step], preferred_element_type=F32)

    right_ref[...] = quarter(1)
    left_ref[...] = quarter(GROUP - 1)
    far = quarter(2)
    far_up_ref[...] = far[:half]
    far_down_ref[...] = far[half:]
    mine_ref[...] = quarter(0)


def product_quarters(sampled, slab):
    (rows, n), width = sampled.shape, slab.shape[1] // GROUP
    whole = jax.ShapeDtypeStruct((n, width), F32)
    part = jax.ShapeDtypeStruct((n // 2, width), F32)
    return pl.pallas_call(
        product_kernel,
        out_shape=(whole, whole, whole, part, part),
        in_specs=[pl.BlockSpec(memory_space=pltpu.VMEM), pl.BlockSpec(memory_space=pl.ANY)],
        scratch_shapes=[pltpu.VMEM((GROUP, rows, width), slab.dtype), pltpu.SemaphoreType.DMA((GROUP,))],
        compiler_params=pltpu.CompilerParams(vmem_limit_bytes=PRODUCT_MIB * 2**20),
        cost_estimate=pl.CostEstimate(flops=16 * 10**8, bytes_accessed=6 * 2**20, transcendentals=0),
        name="product_quarters",
    )(sampled, slab)


def shift(x, step):
    size = lax.axis_size("row")
    return lax.ppermute(x, "row", [(i, (i + step) % size) for i in range(size)])


def copies(x, count):
    return jnp.broadcast_to(x[None], (count, *x.shape))


def local(slab, sketch):
    rows, cols = slab.shape
    width = sketch.shape[1]
    col_size, row_size = lax.axis_size("col"), lax.axis_size("row")
    share = rows // col_size
    piece = width // col_size
    out_rows = width // row_size
    with jax.named_scope("sample"):
        partial = jnp.dot(slab, sketch, preferred_element_type=F32)
        sent = (partial * SKETCH_SCALE).astype(F16).reshape(col_size, share, width)
        got = lax.all_to_all(sent, "col", 0, 0)
        own = jnp.sum(got.astype(F32), axis=0) * (1.0 / SKETCH_SCALE)
        shares = lax.all_to_all(copies((own * SAMPLE_SCALE).astype(F16), col_size), "col", 0, 0)
        sampled = shares.reshape(rows, width).astype(F32) * (1.0 / SAMPLE_SCALE)
    with jax.named_scope("gram"):
        part = lax.dot_general(sampled, sampled, (((0,), (0,)), ((), ())), precision=EXACT, preferred_element_type=F32)
        part = lax.dynamic_slice_in_dim(part, lax.axis_index("col") * piece, piece, 0)
        strip = jnp.sum(lax.all_to_all(copies(part, row_size), "row", 0, 0), axis=0)
    with jax.named_scope("product"):
        mine, right, left, far_up, far_down = product_quarters(sampled, slab)
        near = (mine, shift(right, 1), shift(left, -1))
        far_up, far_down, strip = lax.optimization_barrier((far_up, far_down, strip))
        parts = near + (shift(far_up, 2), shift(far_down, -2))
    with jax.named_scope("gram"):
        gram = lax.all_to_all(copies(strip, col_size), "col", 0, 0).reshape(width, width)
    with jax.named_scope("factor"):
        inverse = inverse_factor(gram)
    with jax.named_scope("basis"):
        basis = lax.dot_general(own, inverse, (((1,), (1,)), ((), ())), precision=EXACT, preferred_element_type=F32)
    with jax.named_scope("projected"):
        sent = apply_inverse(inverse, parts).astype(F16).reshape(row_size, out_rows, cols // GROUP)
        got = lax.all_to_all(sent, "row", 0, 0).reshape(row_size // GROUP, GROUP, out_rows, cols // GROUP)
        projected = jnp.sum(got.astype(F32), axis=0) * (1.0 / PROJ_SCALE)
        projected = projected.transpose(1, 0, 2).reshape(out_rows, cols)
    return (basis, projected)


def solution(mesh):
    return jax.shard_map(
        local,
        mesh=mesh,
        in_specs=(P("row", "col"), P("col", None)),
        out_specs=(P(("row", "col"), None), P("row", "col")),
        check_vma=False,
    )
```

```python
import jax
import jax.numpy as jnp
from jax import lax
from jax.experimental import pallas as pl
from jax.experimental.pallas import tpu as pltpu
from jax.sharding import PartitionSpec as P

F32 = jnp.float32
F16 = jnp.float16
BF16 = jnp.bfloat16
EXACT = lax.Precision.HIGHEST
TILE = 64
LANES = 128
PRODUCT_MIB = 50
GROUP = 4
SKETCH_SCALE = 128.0
SAMPLE_SCALE = 4.0
PROJ_SCALE = 128.0


def eliminate(tile, out_ref, n):
    groups = [tile[8 * g : 8 * g + 8, :] for g in range(n // 8)]
    shape = groups[0].shape
    spread = lambda v: jnp.broadcast_to(v, shape)
    for g in range(n // 8):
        j = 8 * g
        later = range(g + 1, n // 8)
        own = [spread(groups[g][:, j + k : j + k + 1]) for k in range(8)]
        cols = {h: [spread(groups[h][:, j + k : j + k + 1]) for k in range(8)] for h in later}
        s = [[spread(own[k][i : i + 1, :]) for k in range(i + 1)] for i in range(8)]
        rows = [spread(groups[g][i : i + 1, :]) for i in range(8)]
        for k in range(0, 8, 2):
            a, b, c = s[k][k], s[k + 1][k], s[k + 1][k + 1]
            det = a * c - b * b
            inv = 1.0 / det
            for i in range(k + 2, 8):
                u0 = c * s[i][k] - b * s[i][k + 1]
                u1 = a * s[i][k + 1] - b * s[i][k]
                for m in range(k + 2, i + 1):
                    s[i][m] = s[i][m] - inv * (u0 * s[m][k] + u1 * s[m][k + 1])
                rows[i] = rows[i] - inv * (u0 * rows[k] + u1 * rows[k + 1])
            for h in later:
                u0 = inv * (c * cols[h][k] - b * cols[h][k + 1])
                u1 = inv * (a * cols[h][k + 1] - b * cols[h][k])
                for m in range(k + 2, 8):
                    cols[h][m] = cols[h][m] - (u0 * s[m][k] + u1 * s[m][k + 1])
                groups[h] = groups[h] - (u0 * rows[k] + u1 * rows[k + 1])
            inv_a = 1.0 / a
            x0 = rows[k] * lax.rsqrt(a)
            x1 = (rows[k + 1] - (b * inv_a) * rows[k]) * lax.rsqrt(det * inv_a)
            out_ref[j + k : j + k + 1, :] = x0[0:1, :]
            out_ref[j + k + 1 : j + k + 2, :] = x1[0:1, :]


def eye(size):
    rows = lax.broadcasted_iota(jnp.int32, (size, size), 0)
    return (rows == lax.broadcasted_iota(jnp.int32, (size, size), 1)).astype(F32)


def factor_kernel(gram_ref, inv_ref, aug, x_ref):
    n = gram_ref.shape[0]
    aug[:, :n] = gram_ref[...]
    aug[:, n:] = eye(n)
    for k in range(n // TILE):
        lo, hi = k * TILE, (k + 1) * TILE
        tile = jnp.concatenate([aug[lo:hi, lo:hi], eye(TILE)], axis=1)
        eliminate(tile, x_ref, TILE)
        first, last = hi // LANES * LANES, n + pl.cdiv(hi, LANES) * LANES
        row = jnp.dot(x_ref[:, TILE:], aug[lo:hi, first:last], precision=EXACT, preferred_element_type=F32)
        inv_ref[lo:hi, : last - n] = row[:, n - first :]
        if last < 2 * n:
            inv_ref[lo:hi, last - n :] = jnp.zeros((TILE, 2 * n - last), F32)
        if hi < n:
            aug[hi:, first:last] = aug[hi:, first:last] - lax.dot_general(
                row[:, hi - first : n - first], row, (((0,), (0,)), ((), ())), precision=EXACT, preferred_element_type=F32
            )


def inverse_factor(gram):
    n = gram.shape[0]
    return pl.pallas_call(
        factor_kernel,
        out_shape=jax.ShapeDtypeStruct((n, n), F32),
        scratch_shapes=[pltpu.VMEM((n, 2 * n), F32), pltpu.VMEM((TILE, 2 * TILE), F32)],
        compiler_params=pltpu.CompilerParams(vmem_limit_bytes=16 * 2**20),
        cost_estimate=pl.CostEstimate(flops=10**8, bytes_accessed=2**20, transcendentals=0),
        name="inverse_factor",
    )(gram)


def apply_kernel(inv_ref, mine_ref, left_ref, right_ref, up_ref, down_ref, proj_ref, down, sem):
    load = pltpu.make_async_copy(down_ref, down, sem)
    load.start()
    split = up_ref.shape[0]
    near = mine_ref[...] + left_ref[...] + right_ref[...]
    upper = near[:split] + up_ref[...]
    first = jnp.dot(inv_ref[:, :split], upper, precision=EXACT, preferred_element_type=F32)
    load.wait()
    rest = near[split:] + down[...]
    second = jnp.dot(inv_ref[:, split:], rest, precision=EXACT, preferred_element_type=F32)
    proj_ref[...] = (first + second) * PROJ_SCALE


def apply_inverse(inverse, parts):
    whole, last = pl.BlockSpec(memory_space=pltpu.VMEM), parts[-1]
    return pl.pallas_call(
        apply_kernel,
        out_shape=jax.ShapeDtypeStruct(parts[0].shape, F32),
        in_specs=[whole] * len(parts) + [pl.BlockSpec(memory_space=pl.ANY)],
        scratch_shapes=[pltpu.VMEM(last.shape, F32), pltpu.SemaphoreType.DMA],
        compiler_params=pltpu.CompilerParams(vmem_limit_bytes=16 * 2**20),
        cost_estimate=pl.CostEstimate(flops=6 * 10**8, bytes_accessed=3 * 2**20, transcendentals=0),
        name="apply_inverse",
    )(inverse, *parts)


def product_kernel(sampled_ref, slab_ref, mine_ref, right_ref, left_ref, far_up_ref, far_down_ref, held, sems):
    split, width = far_up_ref.shape
    at = lax.axis_index("row")

    def load(step):
        start = pl.multiple_of(lax.rem(at + step, GROUP) * width, width)
        return pltpu.make_async_copy(slab_ref.at[:, pl.ds(start, width)], held.at[step], sems.at[step])

    order = (1, 3, 2, 0)
    for step in order:
        load(step).start()
    sampled = sampled_ref[...].T
    high = sampled.astype(BF16)
    low = (sampled - high.astype(F32)).astype(BF16)

    def quarter(step):
        load(step).wait()
        total = jnp.dot(high, held[step], preferred_element_type=F32)
        return total + jnp.dot(low, held[step], preferred_element_type=F32)

    right_ref[...] = quarter(1)
    left_ref[...] = quarter(GROUP - 1)
    far = quarter(2)
    far_up_ref[...] = far[:split]
    far_down_ref[...] = far[split:]
    mine_ref[...] = quarter(0)


def product_quarters(sampled, slab):
    (rows, n), width = sampled.shape, slab.shape[1] // GROUP
    whole = jax.ShapeDtypeStruct((n, width), F32)
    upper = jax.ShapeDtypeStruct((n // 2, width), F32)
    lower = jax.ShapeDtypeStruct((n // 2, width), F32)
    return pl.pallas_call(
        product_kernel,
        out_shape=(whole, whole, whole, upper, lower),
        in_specs=[pl.BlockSpec(memory_space=pltpu.VMEM), pl.BlockSpec(memory_space=pl.ANY)],
        scratch_shapes=[pltpu.VMEM((GROUP, rows, width), slab.dtype), pltpu.SemaphoreType.DMA((GROUP,))],
        compiler_params=pltpu.CompilerParams(vmem_limit_bytes=PRODUCT_MIB * 2**20),
        cost_estimate=pl.CostEstimate(flops=16 * 10**8, bytes_accessed=6 * 2**20, transcendentals=0),
        name="product_quarters",
    )(sampled, slab)


def shift(x, step):
    size = lax.axis_size("row")
    return lax.ppermute(x, "row", [(i, (i + step) % size) for i in range(size)])


def copies(x, count):
    return jnp.broadcast_to(x[None], (count, *x.shape))


def local(slab, sketch):
    rows, cols = slab.shape
    width = sketch.shape[1]
    col_size, row_size = lax.axis_size("col"), lax.axis_size("row")
    share = rows // col_size
    piece = width // col_size
    out_rows = width // row_size
    with jax.named_scope("sample"):
        partial = jnp.dot(slab, sketch, preferred_element_type=F32)
        sent = (partial * SKETCH_SCALE).astype(F16).reshape(col_size, share, width)
        got = lax.all_to_all(sent, "col", 0, 0)
        own = jnp.sum(got.astype(F32), axis=0) * (1.0 / SKETCH_SCALE)
        shares = lax.all_to_all(copies((own * SAMPLE_SCALE).astype(F16), col_size), "col", 0, 0)
        sampled = shares.reshape(rows, width).astype(F32) * (1.0 / SAMPLE_SCALE)
    with jax.named_scope("gram"):
        part = lax.dot_general(sampled, sampled, (((0,), (0,)), ((), ())), precision=EXACT, preferred_element_type=F32)
        part = lax.dynamic_slice_in_dim(part, lax.axis_index("col") * piece, piece, 0)
        strip = jnp.sum(lax.all_to_all(copies(part, row_size), "row", 0, 0), axis=0)
    with jax.named_scope("product"):
        mine, right, left, far_up, far_down = product_quarters(sampled, slab)
        near = (mine, shift(right, 1), shift(left, -1))
        far_up, far_down, strip = lax.optimization_barrier((far_up, far_down, strip))
        parts = near + (shift(far_up, 2), shift(far_down, -2))
    with jax.named_scope("gram"):
        gram = lax.all_to_all(copies(strip, col_size), "col", 0, 0).reshape(width, width)
    with jax.named_scope("factor"):
        inverse = inverse_factor(gram)
    with jax.named_scope("basis"):
        basis = lax.dot_general(own, inverse, (((1,), (1,)), ((), ())), precision=EXACT, preferred_element_type=F32)
    with jax.named_scope("projected"):
        sent = apply_inverse(inverse, parts).astype(F16).reshape(row_size, out_rows, cols // GROUP)
        got = lax.all_to_all(sent, "row", 0, 0).reshape(row_size // GROUP, GROUP, out_rows, cols // GROUP)
        projected = jnp.sum(got.astype(F32), axis=0) * (1.0 / PROJ_SCALE)
        projected = projected.transpose(1, 0, 2).reshape(out_rows, cols)
    return (basis, projected)


def solution(mesh):
    return jax.shard_map(
        local,
        mesh=mesh,
        in_specs=(P("row", "col"), P("col", None)),
        out_specs=(P(("row", "col"), None), P("row", "col")),
        check_vma=False,
    )
```

```python
import jax
import jax.numpy as jnp
from jax import lax
from jax.experimental import pallas as pl
from jax.experimental.pallas import tpu as pltpu
from jax.sharding import PartitionSpec as P

F32 = jnp.float32
F16 = jnp.float16
BF16 = jnp.bfloat16
EXACT = lax.Precision.HIGHEST
TILE = 64
LANES = 128
PRODUCT_MIB = 50
GROUP = 4
SKETCH_SCALE = 128.0
SAMPLE_SCALE = 4.0
PROJ_SCALE = 128.0


def eliminate(tile, out_ref, n):
    groups = [tile[8 * g : 8 * g + 8, :] for g in range(n // 8)]
    shape = groups[0].shape
    spread = lambda v: jnp.broadcast_to(v, shape)
    for g in range(n // 8):
        j = 8 * g
        later = range(g + 1, n // 8)
        own = [spread(groups[g][:, j + k : j + k + 1]) for k in range(8)]
        cols = {h: [spread(groups[h][:, j + k : j + k + 1]) for k in range(8)] for h in later}
        s = [[spread(own[k][i : i + 1, :]) for k in range(i + 1)] for i in range(8)]
        rows = [spread(groups[g][i : i + 1, :]) for i in range(8)]
        for k in range(0, 8, 2):
            a, b, c = s[k][k], s[k + 1][k], s[k + 1][k + 1]
            det = a * c - b * b
            inv = 1.0 / det
            for i in range(k + 2, 8):
                u0 = c * s[i][k] - b * s[i][k + 1]
                u1 = a * s[i][k + 1] - b * s[i][k]
                for m in range(k + 2, i + 1):
                    s[i][m] = s[i][m] - inv * (u0 * s[m][k] + u1 * s[m][k + 1])
                rows[i] = rows[i] - inv * (u0 * rows[k] + u1 * rows[k + 1])
            for h in later:
                u0 = inv * (c * cols[h][k] - b * cols[h][k + 1])
                u1 = inv * (a * cols[h][k + 1] - b * cols[h][k])
                for m in range(k + 2, 8):
                    cols[h][m] = cols[h][m] - (u0 * s[m][k] + u1 * s[m][k + 1])
                groups[h] = groups[h] - (u0 * rows[k] + u1 * rows[k + 1])
            inv_a = 1.0 / a
            x0 = rows[k] * lax.rsqrt(a)
            x1 = (rows[k + 1] - (b * inv_a) * rows[k]) * lax.rsqrt(det * inv_a)
            out_ref[j + k : j + k + 1, :] = x0[0:1, :]
            out_ref[j + k + 1 : j + k + 2, :] = x1[0:1, :]


def eye(size):
    rows = lax.broadcasted_iota(jnp.int32, (size, size), 0)
    return (rows == lax.broadcasted_iota(jnp.int32, (size, size), 1)).astype(F32)


def factor_kernel(gram_ref, inv_ref, aug, x_ref):
    n = gram_ref.shape[0]
    aug[:, :n] = gram_ref[...]
    aug[:, n:] = eye(n)
    for k in range(n // TILE):
        lo, hi = k * TILE, (k + 1) * TILE
        tile = jnp.concatenate([aug[lo:hi, lo:hi], eye(TILE)], axis=1)
        eliminate(tile, x_ref, TILE)
        first, last = hi // LANES * LANES, n + pl.cdiv(hi, LANES) * LANES
        row = jnp.dot(x_ref[:, TILE:], aug[lo:hi, first:last], precision=EXACT, preferred_element_type=F32)
        inv_ref[lo:hi, : last - n] = row[:, n - first :]
        if last < 2 * n:
            inv_ref[lo:hi, last - n :] = jnp.zeros((TILE, 2 * n - last), F32)
        if hi < n:
            aug[hi:, first:last] = aug[hi:, first:last] - lax.dot_general(
                row[:, hi - first : n - first], row, (((0,), (0,)), ((), ())), precision=EXACT, preferred_element_type=F32
            )


def inverse_factor(gram):
    n = gram.shape[0]
    return pl.pallas_call(
        factor_kernel,
        out_shape=jax.ShapeDtypeStruct((n, n), F32),
        scratch_shapes=[pltpu.VMEM((n, 2 * n), F32), pltpu.VMEM((TILE, 2 * TILE), F32)],
        compiler_params=pltpu.CompilerParams(vmem_limit_bytes=16 * 2**20),
        cost_estimate=pl.CostEstimate(flops=10**9, bytes_accessed=2**20, transcendentals=0),
        name="inverse_factor",
    )(gram)


def apply_kernel(inv_ref, mine_ref, left_ref, right_ref, up_ref, down_ref, proj_ref):
    split = up_ref.shape[0]
    near = mine_ref[...] + left_ref[...] + right_ref[...]
    total = jnp.concatenate([near[:split] + up_ref[...], near[split:] + down_ref[...]], axis=0)
    proj_ref[...] = jnp.dot(inv_ref[...], total, precision=EXACT, preferred_element_type=F32) * PROJ_SCALE


def apply_inverse(inverse, parts):
    return pl.pallas_call(
        apply_kernel,
        out_shape=jax.ShapeDtypeStruct(parts[0].shape, F32),
        compiler_params=pltpu.CompilerParams(vmem_limit_bytes=16 * 2**20),
        cost_estimate=pl.CostEstimate(flops=6 * 10**8, bytes_accessed=3 * 2**20, transcendentals=0),
        name="apply_inverse",
    )(inverse, *parts)


def product_kernel(sampled_ref, slab_ref, mine_ref, right_ref, left_ref, far_up_ref, far_down_ref, held, sems):
    split, width = far_up_ref.shape
    at = lax.axis_index("row")

    def load(step):
        start = pl.multiple_of(lax.rem(at + step, GROUP) * width, width)
        return pltpu.make_async_copy(slab_ref.at[:, pl.ds(start, width)], held.at[step], sems.at[step])

    order = (1, 3, 2, 0)
    for step in order:
        load(step).start()
    sampled = sampled_ref[...].T
    high = sampled.astype(BF16)
    low = (sampled - high.astype(F32)).astype(BF16)

    def quarter(step):
        load(step).wait()
        total = jnp.dot(high, held[step], preferred_element_type=F32)
        return total + jnp.dot(low, held[step], preferred_element_type=F32)

    right_ref[...] = quarter(1)
    left_ref[...] = quarter(GROUP - 1)
    far = quarter(2)
    far_up_ref[...] = far[:split]
    far_down_ref[...] = far[split:]
    mine_ref[...] = quarter(0)


def product_quarters(sampled, slab):
    (rows, n), width = sampled.shape, slab.shape[1] // GROUP
    whole = jax.ShapeDtypeStruct((n, width), F32)
    upper = jax.ShapeDtypeStruct((n * 5 // 8, width), F32)
    lower = jax.ShapeDtypeStruct((n * 3 // 8, width), F32)
    return pl.pallas_call(
        product_kernel,
        out_shape=(whole, whole, whole, upper, lower),
        in_specs=[pl.BlockSpec(memory_space=pltpu.VMEM), pl.BlockSpec(memory_space=pl.ANY)],
        scratch_shapes=[pltpu.VMEM((GROUP, rows, width), slab.dtype), pltpu.SemaphoreType.DMA((GROUP,))],
        compiler_params=pltpu.CompilerParams(vmem_limit_bytes=PRODUCT_MIB * 2**20),
        cost_estimate=pl.CostEstimate(flops=16 * 10**8, bytes_accessed=6 * 2**20, transcendentals=0),
        name="product_quarters",
    )(sampled, slab)


def shift(x, step):
    size = lax.axis_size("row")
    return lax.ppermute(x, "row", [(i, (i + step) % size) for i in range(size)])


def copies(x, count):
    return jnp.broadcast_to(x[None], (count, *x.shape))


def local(slab, sketch):
    rows, cols = slab.shape
    width = sketch.shape[1]
    col_size, row_size = lax.axis_size("col"), lax.axis_size("row")
    share = rows // col_size
    piece = width // col_size
    out_rows = width // row_size
    with jax.named_scope("sample"):
        partial = jnp.dot(slab, sketch, preferred_element_type=F32)
        sent = (partial * SKETCH_SCALE).astype(F16).reshape(col_size, share, width)
        got = lax.all_to_all(sent, "col", 0, 0)
        own = jnp.sum(got.astype(F32), axis=0) * (1.0 / SKETCH_SCALE)
        shares = lax.all_to_all(copies((own * SAMPLE_SCALE).astype(F16), col_size), "col", 0, 0)
        sampled = shares.reshape(rows, width).astype(F32) * (1.0 / SAMPLE_SCALE)
    with jax.named_scope("gram"):
        part = lax.dot_general(sampled, sampled, (((0,), (0,)), ((), ())), precision=EXACT, preferred_element_type=F32)
        part = lax.dynamic_slice_in_dim(part, lax.axis_index("col") * piece, piece, 0)
        strip = jnp.sum(lax.all_to_all(copies(part, row_size), "row", 0, 0), axis=0)
    with jax.named_scope("product"):
        mine, right, left, far_up, far_down = product_quarters(sampled, slab)
        near = (mine, shift(right, 1), shift(left, -1))
        far_up, far_down, strip = lax.optimization_barrier((far_up, far_down, strip))
        parts = near + (shift(far_up, 2), shift(far_down, -2))
    with jax.named_scope("gram"):
        gram = lax.all_to_all(copies(strip, col_size), "col", 0, 0).reshape(width, width)
    with jax.named_scope("factor"):
        inverse = inverse_factor(gram)
    with jax.named_scope("basis"):
        basis = lax.dot_general(own, inverse, (((1,), (1,)), ((), ())), precision=EXACT, preferred_element_type=F32)
    with jax.named_scope("projected"):
        sent = apply_inverse(inverse, parts).astype(F16).reshape(row_size, out_rows, cols // GROUP)
        got = lax.all_to_all(sent, "row", 0, 0).reshape(row_size // GROUP, GROUP, out_rows, cols // GROUP)
        projected = jnp.sum(got.astype(F32), axis=0) * (1.0 / PROJ_SCALE)
        projected = projected.transpose(1, 0, 2).reshape(out_rows, cols)
    return (basis, projected)


def solution(mesh):
    return jax.shard_map(
        local,
        mesh=mesh,
        in_specs=(P("row", "col"), P("col", None)),
        out_specs=(P(("row", "col"), None), P("row", "col")),
        check_vma=False,
    )
```
